32 devices in a mesh: groups: 2 (over y), seq: 4 (over z), head: 2 (over x), sub: 2 (over core).
Axes of the slice: x: 2, y: 2, z: 4, core: 2. Of those that a mesh axis runs over, the one named last changes fastest.
Arguments:
- queries: bfloat16 [8192, 2048], P(('groups', 'seq', 'sub'), 'head'), parts along dimension 0, may hold values from -4.5 to 4.5
- keys: bfloat16 [8192, 2048], P(('groups', 'seq', 'sub'), 'head'), parts along dimension 0, may hold values from -4.5 to 4.5
- values: bfloat16 [8192, 2048], P(('groups', 'seq', 'sub'), 'head'), parts along dimension 0, may hold values from -6 to 6
- grad_out: bfloat16 [8192, 2048], P(('groups', 'seq', 'sub'), 'head'), parts along dimension 0, may hold values from -6 to 6
- cluster_ids: int32 [16, 8192, 1], P('head', ('groups', 'seq', 'sub')), parts along dimension 1, may hold values from 0 to 63; in each aligned block of 512 rows (0 to 511, 512 to 1023, ..., all dimensions but the last counted through in order) at most 12 rows name the same one
Outputs:
- attention: bfloat16 [8192, 2048], P(('groups', 'seq', 'sub'), 'head'), parts along dimension 0
- grad_queries: bfloat16 [8192, 2048], P(('groups', 'seq', 'sub'), 'head'), parts along dimension 0
- grad_keys: bfloat16 [8192, 2048], P(('groups', 'seq', 'sub'), 'head'), parts along dimension 0
- grad_values: bfloat16 [8192, 2048], P(('groups', 'seq', 'sub'), 'head'), parts along dimension 0
- centroid_sums: float32 [16, 128, 128], P('head', 'groups'), parts along dimension 1
The draws below stay inside these ranges and needn't reach their ends.
There are 2 independent parts, one for each index of `groups`. The reference program is written for one: setup_inputs(seed, part) draws one part's arguments, and reference() takes and returns one part's arrays. A program takes and returns all parts, laid end to end along the dimension named above; each array names one. Nothing has to cross between parts.
Inputs may be any that keep to these rules, and one draw needn't show every extreme that they name: `cluster_ids`: in each head, the tokens of one device (aligned blocks of 512 tokens) name one cluster at most 12 times, a bound that some block reaches.
All inputs are finite; a program needn't handle non-finite values.
Results may differ from the reference program's by a relative error of at most 0.0052.
Values may be sent and summed in bfloat16 or wider, within the bound.
A program may use at most 128 MiB of HBM per device.

```python
import math
import jax
import jax.numpy as jnp
import numpy as np
from jax import lax

HEADS = 16
HEAD_DIM = 128
CLUSTERS = 64
TOK_DEV = 512
CAP = 12
TOKENS = 4096
ROWS_CL = 96


def shared_law(key):
    drawn = jnp.clip(jax.random.normal(key, (TOKENS, HEADS * HEAD_DIM)), -4.5, 4.5)
    return drawn.astype(jnp.bfloat16)


def draw_queries(key, part):
    key = jax.random.fold_in(key, 1)
    return shared_law(key)


def draw_keys(key, part):
    key = jax.random.fold_in(key, 3)
    return shared_law(key)


def level_of(stream_key, shape, pieces, smallest, largest):
    def one(position, parts):
        steps = jax.random.uniform(jax.random.fold_in(jax.random.fold_in(stream_key, 6), position), (parts,), jnp.float32, smallest / len(pieces), largest / len(pieces))
        return jnp.repeat(jnp.exp(steps), shape[position] // parts).reshape((-1,) + (1,) * (len(shape) - position - 1))

    gain = one(*pieces[0])
    for cut in pieces[1:]:
        gain = gain * one(*cut)
    return gain


def deal_out(stream_key, own, number, rows, count, top, most, slope):
    order = jax.random.permutation(stream_key, count)
    heavy_load, common = portions_of(count, rows * top, most, slope, True), portions_of(count, rows * top, most, slope, False)
    places = jnp.arange(count)

    def named(tallies, offset_by):
        used = int((tallies > 0).sum())
        fixed = max(1, used // 4)
        passed = fixed + (places - fixed + offset_by * (used - fixed)) % max(1, count - fixed)
        return jnp.zeros((count,), jnp.int32).at[order[jnp.where(places < fixed, places, passed)]].set(jnp.asarray(tallies, jnp.int32))

    tallies = jnp.where(number % 4 == 0, named(heavy_load, number // 4), named(common, number - number // 4 - 1))
    mixed = jax.random.permutation(jax.random.fold_in(own, 3), count)
    donor, taker = mixed[0:count // 2 * 2:2], mixed[1:count // 2 * 2:2]
    margin = jnp.minimum(tallies[donor] - 1, most - tallies[taker]) // 2
    margin = jnp.where((donor == order[0]) | (taker == order[0]) | (tallies[taker] == 0), 0, jnp.maximum(margin, 0))
    passed = jax.random.randint(jax.random.fold_in(own, 4), (count // 2,), 0, 1 << 20) % (margin + 1)
    tallies = tallies.at[donor].add(-passed).at[taker].add(passed)
    items = jnp.searchsorted(jnp.cumsum(tallies), jnp.arange(rows * top), side="right").astype(jnp.int32)
    grid = items.reshape(top, rows).T
    grid = grid[jax.random.permutation(jax.random.fold_in(own, 1), rows)]
    offset_by = jax.random.randint(jax.random.fold_in(own, 2), (rows, 1), 0, top)
    return jnp.take_along_axis(grid, (jnp.arange(top)[None, :] + offset_by) % top, axis=1)


def portions_of(amount, total, reach, slope, full):
    portions = [(1 << 20) // math.isqrt(rank ** slope) + 1 for rank in range(1, amount + 1)]
    largest = reach if full else min(reach, max(-(-total // amount), total * portions[0] // sum(portions)))
    least = 1 if total - largest >= amount - 1 else 0
    counts, surplus = [largest] + [least] * (amount - 1), total - largest - least * (amount - 1)
    while surplus > 0:
        candidates = [i for i in range(1, amount) if counts[i] < largest] or [i for i in range(1, amount) if counts[i] < reach]
        pool, left = sum([portions[i] for i in candidates]), surplus
        for i in candidates:
            addition = min(reach - counts[i], max(1, left * portions[i] // pool), surplus)
            counts[i] = counts[i] + addition
            surplus = surplus - addition
    return np.array(counts)


def noise(rng, dims, spread, most, shards=(), kind=jnp.bfloat16):
    values = spread * jax.random.normal(rng, dims, jnp.float32)
    if shards:
        values = values * level_of(rng, dims, shards, -0.22, 0.18)
    return jnp.clip(values, -most, most).astype(kind)


def setup_inputs(seed: int = 0, part: int = 0) -> dict:
    key_of = jax.random.split(jax.random.key(seed), 6)
    part_keys = jax.random.split(jax.random.fold_in(key_of[5], part), 6)
    queries = draw_queries(jax.random.fold_in(jax.random.fold_in(key_of[5], part), 71), part)
    keys = draw_keys(jax.random.fold_in(jax.random.fold_in(key_of[5], part), 71), part)
    values = noise(part_keys[2], (TOKENS, HEADS * HEAD_DIM), 1.0, 6.0, ((0, 8), (1, 2)))
    grad_out = noise(part_keys[3], (TOKENS, HEADS * HEAD_DIM), 1.0, 6.0, ((0, 8), (1, 2)))
    cluster_ids_keys = jax.random.split(jax.random.fold_in(part_keys[4], 1), HEADS * TOKENS // TOK_DEV)
    cluster_ids_turns = jax.random.permutation(jax.random.fold_in(part_keys[4], 3), HEADS * TOKENS // TOK_DEV)
    cluster_ids = jax.vmap(lambda own, number: deal_out(jax.random.fold_in(part_keys[4], 2), own, number, TOK_DEV, CLUSTERS, 1, CAP, 2))(cluster_ids_keys, cluster_ids_turns).reshape((HEADS, TOKENS, 1))
    return dict(queries=queries, keys=keys, values=values, grad_out=grad_out, cluster_ids=cluster_ids)


norm_eps = 1e-06
masked_score = -1e+30

def cluster_block(query_rows, key_rows, value_rows, grad_rows, filled_slot):
    score_scale = HEAD_DIM ** (-0.5)
    scores = jnp.dot(query_rows, key_rows.T, preferred_element_type=jnp.float32) * score_scale
    scores = jnp.where(filled_slot[None, :], scores, masked_score)
    row_max = lax.optimization_barrier(jnp.max(scores, axis=-1, keepdims=True))
    exp_scores = jnp.exp(scores - row_max)
    probabilities = exp_scores / lax.optimization_barrier(jnp.sum(exp_scores, axis=-1, keepdims=True))
    weights = probabilities.astype(jnp.bfloat16)
    attention = jnp.dot(weights, value_rows, preferred_element_type=jnp.float32).astype(jnp.bfloat16)
    dprobs = jnp.dot(grad_rows, value_rows.T, preferred_element_type=jnp.float32)
    row_delta = lax.optimization_barrier(jnp.sum(probabilities * dprobs, axis=-1, keepdims=True))
    dscore = (score_scale * probabilities * (dprobs - row_delta)).astype(jnp.bfloat16)
    dquery = jnp.dot(dscore, key_rows, preferred_element_type=jnp.float32).astype(jnp.bfloat16)
    dkey = jnp.dot(dscore.T, query_rows, preferred_element_type=jnp.float32).astype(jnp.bfloat16)
    dvalue = jnp.dot(weights.T, grad_rows, preferred_element_type=jnp.float32).astype(jnp.bfloat16)
    return jnp.stack([attention, dquery, dkey, dvalue], axis=1)

def reference(queries, keys, values, grad_out, cluster_ids):
    shape_three = (TOKENS, HEADS, HEAD_DIM)
    query_h = jnp.swapaxes(queries.reshape(shape_three), 0, 1)
    key_h = jnp.swapaxes(keys.reshape(shape_three), 0, 1)
    value_h = jnp.swapaxes(values.reshape(shape_three), 0, 1)
    grad_h = jnp.swapaxes(grad_out.reshape(shape_three), 0, 1)

    def one_head(inputs):
        query_one, key_one, value_one, grad_one, cluster_of = inputs

        def one_cluster(cluster):
            cluster_order = jnp.argsort((cluster_of != cluster).astype(jnp.int32), stable=True)[:ROWS_CL].astype(jnp.int32)
            filled_slot = cluster_of[cluster_order] == cluster
            grad_rows = jnp.where(filled_slot[:, None], grad_one[cluster_order], jnp.zeros((), grad_one.dtype))
            block = cluster_block(query_one[cluster_order], key_one[cluster_order], value_one[cluster_order], grad_rows, filled_slot)
            return (cluster_order, filled_slot, block)
        orders, filled, blocks = lax.map(one_cluster, jnp.arange(CLUSTERS, dtype=jnp.int32))
        kept = jnp.where(filled[:, :, None, None], blocks.astype(jnp.float32), jnp.zeros((), jnp.float32))
        total = jnp.zeros((TOKENS, 4, HEAD_DIM), jnp.float32).at[orders.reshape(-1)].add(kept.reshape(-1, 4, HEAD_DIM))
        return total.astype(jnp.bfloat16)
    results = lax.map(one_head, (query_h, key_h, value_h, grad_h, cluster_ids[:, :, 0]))
    results = jnp.swapaxes(results, 0, 1)
    flat_shape = (TOKENS, HEADS * HEAD_DIM)
    attention = results[:, :, 0, :].reshape(flat_shape)
    grad_queries = results[:, :, 1, :].reshape(flat_shape)
    grad_keys = results[:, :, 2, :].reshape(flat_shape)
    grad_values = results[:, :, 3, :].reshape(flat_shape)
    key_float = keys.reshape(shape_three).astype(jnp.float32)
    unit_keys = key_float * lax.rsqrt(lax.optimization_barrier(jnp.sum(key_float * key_float, axis=-1, keepdims=True)) + norm_eps)
    centroid_sums = jax.vmap(lambda values_in, segment_ids: jax.ops.segment_sum(values_in, segment_ids, CLUSTERS), in_axes=(1, 0))(unit_keys, cluster_ids[:, :, 0])
    return (attention, grad_queries, grad_keys, grad_values, centroid_sums)
```

```python
import functools
import jax
import jax.numpy as jnp
from jax import lax
from jax.experimental import pallas as pl
from jax.experimental.pallas import tpu as pltpu
from jax.sharding import PartitionSpec as P

CLUSTERS = 64
CAP = 12
SLOT = 16
AXES = ("seq", "sub")
VMEM = 56 * 1024 * 1024


norm_eps = 1e-06
masked_score = -1e30


def unit_rows(matrix):
    return matrix * lax.rsqrt(jnp.sum(matrix * matrix, axis=-1, keepdims=True) + norm_eps)


def cluster_work(packed, counts):
    head_width = packed.shape[-1] // 4
    row_count = packed.shape[2]
    slot_rank = (jnp.arange(row_count) % CAP).astype(jnp.float32)
    filled = jnp.repeat(counts.astype(jnp.float32), CAP, axis=2)
    filled_slot = slot_rank[None, None, :] < filled
    query_rows = packed[..., :head_width]
    key_rows = packed[..., head_width : 2 * head_width]
    value_rows = packed[..., 2 * head_width : 3 * head_width]
    grad_rows = packed[..., 3 * head_width :]
    score_scale = head_width ** (-0.5)
    scores = (
        jnp.einsum("hcqd,hckd->hcqk", query_rows, key_rows, preferred_element_type=jnp.float32)
        * score_scale
    )
    scores = jnp.where(filled_slot[:, :, None, :], scores, masked_score)
    row_max = jnp.max(scores, axis=-1, keepdims=True)
    exp_scores = jnp.exp(scores - row_max)
    probabilities = exp_scores / jnp.sum(exp_scores, axis=-1, keepdims=True)
    weights = probabilities.astype(jnp.bfloat16)
    attention = jnp.einsum(
        "hcqk,hckd->hcqd", weights, value_rows, preferred_element_type=jnp.float32
    ).astype(jnp.bfloat16)
    dprobs = jnp.einsum(
        "hcqd,hckd->hcqk", grad_rows, value_rows, preferred_element_type=jnp.float32
    )
    row_delta = jnp.sum(probabilities * dprobs, axis=-1, keepdims=True)
    dscore = (score_scale * probabilities * (dprobs - row_delta)).astype(jnp.bfloat16)
    dquery = jnp.einsum(
        "hcqk,hckd->hcqd", dscore, key_rows, preferred_element_type=jnp.float32
    ).astype(jnp.bfloat16)
    dkey = jnp.einsum(
        "hcqk,hcqd->hckd", dscore, query_rows, preferred_element_type=jnp.float32
    ).astype(jnp.bfloat16)
    dvalue = jnp.einsum(
        "hcqk,hcqd->hckd", weights, grad_rows, preferred_element_type=jnp.float32
    ).astype(jnp.bfloat16)
    result = jnp.concatenate([attention, dquery, dkey, dvalue], axis=-1)
    cluster_sums = None
    return (result, cluster_sums)


def padded_path(queries, keys, values, grad_out, cluster_ids):
    tok_rows = queries.shape[0]
    heads_here = cluster_ids.shape[0]
    head_width = queries.shape[1] // heads_here
    cluster_of = cluster_ids[:, :, 0]
    member = (
        cluster_of[:, :, None] == jnp.arange(CLUSTERS, dtype=jnp.int32)[None, None, :]
    ).astype(jnp.int32)
    before = jnp.cumsum(member, axis=1) - member
    slot_rank = jnp.sum(before * member, axis=2)
    slot_index = cluster_of * CAP + slot_rank
    dispatch = (
        slot_index[:, None, :] == jnp.arange(CLUSTERS * CAP, dtype=jnp.int32)[None, :, None]
    ).astype(jnp.bfloat16)
    counts = jnp.sum(member, axis=1).astype(jnp.bfloat16)[:, :, None]
    head_shape = (tok_rows, heads_here, head_width)
    stacked = jnp.stack(
        [
            queries.reshape(head_shape),
            keys.reshape(head_shape),
            values.reshape(head_shape),
            grad_out.reshape(head_shape),
        ],
        axis=2,
    )
    packed = jnp.einsum(
        "hst,thfd->hsfd", dispatch, stacked, preferred_element_type=jnp.float32
    ).astype(jnp.bfloat16)
    packed = packed.reshape(heads_here, CLUSTERS, CAP, 4 * head_width)
    result, _ = cluster_work(
        lax.all_to_all(packed, AXES, split_axis=1, concat_axis=2, tiled=True),
        lax.all_to_all(counts, AXES, split_axis=1, concat_axis=2, tiled=True),
    )
    sent_back = lax.all_to_all(result, AXES, split_axis=2, concat_axis=1, tiled=True)
    rows_back = sent_back.reshape(heads_here, CLUSTERS * CAP, 4, head_width)
    merged = jnp.einsum(
        "hst,hsfd->thfd", dispatch, rows_back, preferred_element_type=jnp.float32
    ).astype(jnp.bfloat16)
    flat_shape = (tok_rows, heads_here * head_width)
    return tuple(merged[:, :, i, :].reshape(flat_shape) for i in range(4))


def up16(x):
    return -(-x // 16) * 16


def one_hot(hit):
    return jnp.where(hit, 1.0, 0.0).astype(jnp.bfloat16)


def dot(a, b, ca=1, cb=0):
    return lax.dot_general(
        a, b, (((ca,), (cb,)), ((), ())), preferred_element_type=jnp.float32
    )


def pack_kernel(n, hc, width, window, room,
                q_ref, k_ref, v_ref, g_ref, pos_ref, tgt_ref, cnt_ref, out_ref, win):
    tokens = q_ref.shape[0]
    slot = lax.broadcasted_iota(jnp.int32, (n * window, tokens), 0)
    for h in range(hc):
        cols = slice(h * width, (h + 1) * width)
        rows = jnp.concatenate(
            [q_ref[:, cols], k_ref[:, cols], v_ref[:, cols], g_ref[:, cols]], axis=1
        )
        got = dot(one_hot(slot == pos_ref[h]), rows).astype(jnp.bfloat16)
        win[:, h * window:(h + 1) * window, :] = got.reshape(n, window, 4 * width)
    place = lax.broadcasted_iota(jnp.int32, (room, hc * window), 0)
    last = lax.broadcasted_iota(jnp.int32, (room, 4 * width), 0) == room - 1

    def to_owner(o, carry):
        rows = dot(one_hot(place == tgt_ref[o]), win[o])
        out_ref[o] = jnp.where(last, cnt_ref[o], rows).astype(jnp.bfloat16)
        return carry

    lax.fori_loop(0, n, to_owner, 0)


def work_kernel(n, blocks, width, room,
                recv_ref, col_ref, row_ref, valid_ref, out_ref, x, r):
    slots = blocks * SLOT
    scale = width ** (-0.5)
    lane = lax.broadcasted_iota(jnp.int32, (slots, room), 1)
    sublane = lax.broadcasted_iota(jnp.int32, (room, slots), 0)

    def take(s, carry):
        got = dot(one_hot(lane == col_ref[s]), recv_ref[s]).astype(jnp.bfloat16)
        at = pl.ds(pl.multiple_of(s * SLOT, SLOT), SLOT)
        x[:, at, :] = got.reshape(blocks, SLOT, 4 * width)
        return carry

    lax.fori_loop(0, n, take, 0)

    def one(i):
        q = x[i, :, :width]
        k = x[i, :, width:2 * width]
        v = x[i, :, 2 * width:3 * width]
        g = x[i, :, 3 * width:]
        scores = dot(q, k, 1, 1) * scale
        scores = jnp.where(valid_ref[i] > 0, scores, masked_score)
        e = jnp.exp(scores - jnp.max(scores, axis=-1, keepdims=True))
        p = e / jnp.sum(e, axis=-1, keepdims=True)
        w = p.astype(jnp.bfloat16)
        dp = dot(g, v, 1, 1)
        delta = jnp.sum(p * dp, axis=-1, keepdims=True)
        ds = (scale * p * (dp - delta)).astype(jnp.bfloat16)
        r[i, :, :width] = dot(w, v).astype(jnp.bfloat16)
        r[i, :, width:2 * width] = dot(ds, k).astype(jnp.bfloat16)
        r[i, :, 2 * width:3 * width] = dot(ds, q, 0, 0).astype(jnp.bfloat16)
        r[i, :, 3 * width:] = dot(w, g, 0, 0).astype(jnp.bfloat16)

    step = 4 if blocks % 4 == 0 and n * SLOT <= 256 else 1

    def attend(i, carry):
        for j in range(step):
            one(i * step + j)
        return carry

    lax.fori_loop(0, blocks // step, attend, 0)

    def give(s, carry):
        at = pl.ds(pl.multiple_of(s * SLOT, SLOT), SLOT)
        rows = r[:, at, :].reshape(slots, 4 * width)
        out_ref[s] = dot(one_hot(sublane == row_ref[s]), rows).astype(jnp.bfloat16)
        return carry

    lax.fori_loop(0, n, give, 0)


def unpack_kernel(n, hc, width, window, room, earlier, back_ref, pos_ref, tgt_ref, *refs):
    outs, win = refs[earlier:earlier + 4], refs[-1]
    tokens = outs[0].shape[0]
    lane = lax.broadcasted_iota(jnp.int32, (hc * window, room), 1)

    def from_owner(o, carry):
        win[o] = dot(one_hot(lane == tgt_ref[o]), back_ref[o]).astype(jnp.bfloat16)
        return carry

    lax.fori_loop(0, n, from_owner, 0)
    slot = lax.broadcasted_iota(jnp.int32, (tokens, n * window), 1)
    for h in range(hc):
        rows = win[:, h * window:(h + 1) * window, :].reshape(n * window, 4 * width)
        got = dot(one_hot(slot == pos_ref[h]), rows).astype(jnp.bfloat16)
        for f in range(4):
            outs[f][:, h * width:(h + 1) * width] = got[:, f * width:(f + 1) * width]


def full(shape):
    return pl.BlockSpec(shape, lambda i: (0,) * len(shape))


def shards(n, queries, keys, values, grad_out, cluster_ids):
    tok_rows = queries.shape[0]
    heads = cluster_ids.shape[0]
    width = queries.shape[1] // heads
    k = CLUSTERS // n
    chunks = 2 if heads % 2 == 0 else 1
    hc = heads // chunks
    window = up16(k * CAP)
    room = up16(hc * k * CAP * 5 // 6)
    blocks = hc * k
    four = 4 * width
    params = pltpu.CompilerParams(vmem_limit_bytes=VMEM)

    cl = cluster_ids[:, :, 0]
    head_no = jnp.arange(heads, dtype=jnp.int32)[:, None]
    minor = cl // n
    owner = (cl % n + head_no * minor) % n
    cid = owner * k + minor
    names = jnp.arange(CLUSTERS, dtype=jnp.int32)
    member = (cid[:, :, None] == names).astype(jnp.bfloat16)
    tok = jnp.arange(tok_rows)
    earlier = (tok[:, None] > tok[None, :]).astype(jnp.bfloat16)
    before = jnp.einsum("ts,hsc->htc", earlier, member, preferred_element_type=jnp.float32)
    counts = jnp.sum(member.astype(jnp.float32), axis=1)
    same = (names[:, None] // k == names[None, :] // k) & (names[:, None] < names[None, :])
    start = jnp.sum(counts[:, :, None] * same.astype(jnp.float32), axis=1)
    start = start + (names // k * window).astype(jnp.float32)
    pos = jnp.sum(member.astype(jnp.float32) * (before + start[:, None, :]), axis=2)
    pos = pos.astype(jnp.int32)
    seg = jnp.sum(counts.reshape(chunks, hc, n, k), axis=3).astype(jnp.int32)
    ends = jnp.cumsum(seg, axis=1)
    base = ends - seg
    overflow = jnp.max(ends).astype(jnp.int32) > room - 1
    any_overflow = lax.psum(overflow.astype(jnp.float32), tuple(ALL)) > 0
    j = jnp.arange(window, dtype=jnp.int32)
    tgt = jnp.where(j < seg[..., None], base[..., None] + j, -1)
    tgt = jnp.swapaxes(tgt, 1, 2).reshape(chunks, n, hc * window)
    cnt_row = jnp.swapaxes(counts.reshape(chunks, hc, n, k), 1, 2).reshape(chunks, n, 1, blocks)
    cnt_row = jnp.pad(cnt_row, ((0, 0), (0, 0), (0, 0), (0, four - blocks)))

    def pack(c):
        cols = pl.BlockSpec((tok_rows, hc * width), lambda i: (0, c))
        return pl.pallas_call(
            functools.partial(pack_kernel, n, hc, width, window, room),
            grid=(1,),
            out_shape=jax.ShapeDtypeStruct((n, room, four), jnp.bfloat16),
            in_specs=[cols] * 4 + [full((hc, 1, tok_rows)), full((n, 1, hc * window)), full((n, 1, four))],
            out_specs=full((n, room, four)),
            scratch_shapes=[pltpu.VMEM((n, hc * window, four), jnp.bfloat16)],
            compiler_params=params,
            cost_estimate=pl.CostEstimate(flops=6 * 10**9, bytes_accessed=5 * 10**6, transcendentals=0),
        )(queries, keys, values, grad_out,
          pos[c * hc:(c + 1) * hc, None, :], tgt[c][:, None, :], cnt_row[c])

    def work(recv):
        cnt = recv[:, room - 1, :blocks].astype(jnp.float32).astype(jnp.int32)
        lower = jnp.arange(blocks)
        first = jnp.sum(
            jnp.where(lower[:, None] < lower[None, :], cnt[:, :, None], 0), axis=1
        )
        rank = jnp.arange(SLOT, dtype=jnp.int32)
        filled = rank < cnt[..., None]
        source = jnp.where(filled, first[..., None] + rank, -1).reshape(n, blocks * SLOT)
        valid = jnp.swapaxes(filled, 0, 1).reshape(blocks, 1, n * SLOT).astype(jnp.float32)
        return pl.pallas_call(
            functools.partial(work_kernel, n, blocks, width, room),
            out_shape=jax.ShapeDtypeStruct((n, room, four), jnp.bfloat16),
            scratch_shapes=[pltpu.VMEM((blocks, n * SLOT, four), jnp.bfloat16)] * 2,
            compiler_params=params,
            cost_estimate=pl.CostEstimate(flops=10**10, bytes_accessed=5 * 10**6, transcendentals=10**6),
        )(recv, source[:, :, None], source[:, None, :], valid)

    def unpack(c, back, so_far):
        wide = jax.ShapeDtypeStruct((tok_rows, heads * width), jnp.bfloat16)
        cols = pl.BlockSpec((tok_rows, hc * width), lambda i: (0, c))
        return pl.pallas_call(
            functools.partial(unpack_kernel, n, hc, width, window, room, len(so_far)),
            grid=(1,),
            out_shape=[wide] * 4,
            in_specs=[full((n, room, four)), full((hc, tok_rows, 1)), full((n, hc * window, 1))]
            + [pl.BlockSpec(memory_space=pl.ANY)] * len(so_far),
            out_specs=[cols] * 4,
            scratch_shapes=[pltpu.VMEM((n, hc * window, four), jnp.bfloat16)],
            input_output_aliases={3 + i: i for i in range(len(so_far))},
            compiler_params=params,
            cost_estimate=pl.CostEstimate(flops=6 * 10**9, bytes_accessed=5 * 10**6, transcendentals=0),
        )(back, pos[c * hc:(c + 1) * hc, :, None], tgt[c][:, :, None], *so_far)

    def exchange(rows):
        return lax.all_to_all(rows, AXES, split_axis=0, concat_axis=0, tiled=True)

    sent = [exchange(pack(c)) for c in range(chunks)]
    normed = unit_rows(keys.reshape(tok_rows, heads, width).astype(jnp.float32))
    own = (cl[:, :, None] == names).astype(jnp.float32)
    partial_sums = jnp.einsum("htc,thd->hcd", own, normed, precision=lax.Precision.HIGHEST)
    centroid_sums = lax.psum(partial_sums, AXES)
    back = [exchange(work(recv)) for recv in sent]
    outs = ()
    for c in range(chunks - 1):
        outs = unpack(c, back[c], tuple(outs))
    outs = lax.cond(
        any_overflow,
        lambda: padded_path(queries, keys, values, grad_out, cluster_ids),
        lambda: tuple(unpack(chunks - 1, back[-1], tuple(outs))),
    )
    return (*outs, centroid_sums)


ALL = ("groups", "seq", "head", "sub")


def solution(mesh):
    n = mesh.shape["seq"] * mesh.shape["sub"]
    rows = P(("groups", "seq", "sub"), "head")
    return jax.shard_map(
        functools.partial(shards, n),
        mesh=mesh,
        in_specs=(rows, rows, rows, rows, P("head", ("groups", "seq", "sub"), None)),
        out_specs=(rows, rows, rows, rows, P("head", "groups", None)),
        check_vma=False,
    )
```

```python
import functools
import jax
import jax.numpy as jnp
from jax import lax
from jax.experimental import pallas as pl
from jax.experimental.pallas import tpu as pltpu
from jax.sharding import PartitionSpec as P

CLUSTERS = 64
CAP = 12
SLOT = 16
AXES = ("seq", "sub")
VMEM = 56 * 1024 * 1024


norm_eps = 1e-06
masked_score = -1e30


def unit_rows(matrix):
    return matrix * lax.rsqrt(jnp.sum(matrix * matrix, axis=-1, keepdims=True) + norm_eps)


def cluster_work(packed, counts):
    head_width = packed.shape[-1] // 4
    row_count = packed.shape[2]
    slot_rank = (jnp.arange(row_count) % CAP).astype(jnp.float32)
    filled = jnp.repeat(counts.astype(jnp.float32), CAP, axis=2)
    filled_slot = slot_rank[None, None, :] < filled
    query_rows = packed[..., :head_width]
    key_rows = packed[..., head_width : 2 * head_width]
    value_rows = packed[..., 2 * head_width : 3 * head_width]
    grad_rows = packed[..., 3 * head_width :]
    score_scale = head_width ** (-0.5)
    scores = (
        jnp.einsum("hcqd,hckd->hcqk", query_rows, key_rows, preferred_element_type=jnp.float32)
        * score_scale
    )
    scores = jnp.where(filled_slot[:, :, None, :], scores, masked_score)
    row_max = jnp.max(scores, axis=-1, keepdims=True)
    exp_scores = jnp.exp(scores - row_max)
    probabilities = exp_scores / jnp.sum(exp_scores, axis=-1, keepdims=True)
    weights = probabilities.astype(jnp.bfloat16)
    attention = jnp.einsum(
        "hcqk,hckd->hcqd", weights, value_rows, preferred_element_type=jnp.float32
    ).astype(jnp.bfloat16)
    dprobs = jnp.einsum(
        "hcqd,hckd->hcqk", grad_rows, value_rows, preferred_element_type=jnp.float32
    )
    row_delta = jnp.sum(probabilities * dprobs, axis=-1, keepdims=True)
    dscore = (score_scale * probabilities * (dprobs - row_delta)).astype(jnp.bfloat16)
    dquery = jnp.einsum(
        "hcqk,hckd->hcqd", dscore, key_rows, preferred_element_type=jnp.float32
    ).astype(jnp.bfloat16)
    dkey = jnp.einsum(
        "hcqk,hcqd->hckd", dscore, query_rows, preferred_element_type=jnp.float32
    ).astype(jnp.bfloat16)
    dvalue = jnp.einsum(
        "hcqk,hcqd->hckd", weights, grad_rows, preferred_element_type=jnp.float32
    ).astype(jnp.bfloat16)
    result = jnp.concatenate([attention, dquery, dkey, dvalue], axis=-1)
    cluster_sums = None
    return (result, cluster_sums)


def padded_path(queries, keys, values, grad_out, cluster_ids):
    tok_rows = queries.shape[0]
    heads_here = cluster_ids.shape[0]
    head_width = queries.shape[1] // heads_here
    cluster_of = cluster_ids[:, :, 0]
    member = (
        cluster_of[:, :, None] == jnp.arange(CLUSTERS, dtype=jnp.int32)[None, None, :]
    ).astype(jnp.int32)
    before = jnp.cumsum(member, axis=1) - member
    slot_rank = jnp.sum(before * member, axis=2)
    slot_index = cluster_of * CAP + slot_rank
    dispatch = (
        slot_index[:, None, :] == jnp.arange(CLUSTERS * CAP, dtype=jnp.int32)[None, :, None]
    ).astype(jnp.bfloat16)
    counts = jnp.sum(member, axis=1).astype(jnp.bfloat16)[:, :, None]
    head_shape = (tok_rows, heads_here, head_width)
    stacked = jnp.stack(
        [
            queries.reshape(head_shape),
            keys.reshape(head_shape),
            values.reshape(head_shape),
            grad_out.reshape(head_shape),
        ],
        axis=2,
    )
    packed = jnp.einsum(
        "hst,thfd->hsfd", dispatch, stacked, preferred_element_type=jnp.float32
    ).astype(jnp.bfloat16)
    packed = packed.reshape(heads_here, CLUSTERS, CAP, 4 * head_width)
    result, _ = cluster_work(
        lax.all_to_all(packed, AXES, split_axis=1, concat_axis=2, tiled=True),
        lax.all_to_all(counts, AXES, split_axis=1, concat_axis=2, tiled=True),
    )
    sent_back = lax.all_to_all(result, AXES, split_axis=2, concat_axis=1, tiled=True)
    rows_back = sent_back.reshape(heads_here, CLUSTERS * CAP, 4, head_width)
    merged = jnp.einsum(
        "hst,hsfd->thfd", dispatch, rows_back, preferred_element_type=jnp.float32
    ).astype(jnp.bfloat16)
    flat_shape = (tok_rows, heads_here * head_width)
    return tuple(merged[:, :, i, :].reshape(flat_shape) for i in range(4))


def up16(x):
    return -(-x // 16) * 16


def one_hot(hit):
    return jnp.where(hit, 1.0, 0.0).astype(jnp.bfloat16)


def dot(a, b, ca=1, cb=0):
    return lax.dot_general(
        a, b, (((ca,), (cb,)), ((), ())), preferred_element_type=jnp.float32
    )


def pack_kernel(n, hc, width, window, room,
                q_ref, k_ref, v_ref, g_ref, pos_ref, tgt_ref, cnt_ref, out_ref, win):
    tokens = q_ref.shape[0]
    slot = lax.broadcasted_iota(jnp.int32, (n * window, tokens), 0)
    for h in range(hc):
        cols = slice(h * width, (h + 1) * width)
        rows = jnp.concatenate(
            [q_ref[:, cols], k_ref[:, cols], v_ref[:, cols], g_ref[:, cols]], axis=1
        )
        got = dot(one_hot(slot == pos_ref[h]), rows).astype(jnp.bfloat16)
        win[:, h * window:(h + 1) * window, :] = got.reshape(n, window, 4 * width)
    place = lax.broadcasted_iota(jnp.int32, (room, hc * window), 0)
    last = lax.broadcasted_iota(jnp.int32, (room, 4 * width), 0) == room - 1

    def to_owner(o, carry):
        rows = dot(one_hot(place == tgt_ref[o]), win[o])
        out_ref[o] = jnp.where(last, cnt_ref[o], rows).astype(jnp.bfloat16)
        return carry

    lax.fori_loop(0, n, to_owner, 0)


def work_kernel(n, blocks, width, room, recv_ref, out_ref, x, r, from_row, filled):
    slots = blocks * SLOT
    scale = width ** (-0.5)
    sublane = lax.broadcasted_iota(jnp.int32, (room, slots), 0)
    iota = functools.partial(lax.broadcasted_iota, jnp.int32)

    tails = recv_ref[:, room - 16:, :128].reshape(n * 16, 128)
    lane, block = iota((128, slots), 0), iota((128, slots), 1) // SLOT
    count = dot(tails, one_hot(lane == block))
    first = dot(tails, one_hot(lane < block))
    rank = (iota((n * 16, slots), 1) % SLOT).astype(jnp.float32)
    from_row[...] = jnp.where(rank < count, first + rank, -1.0).reshape(n, 16, slots)
    shape = (n * 16, n * SLOT)
    tail_of = one_hot(iota(shape, 0) == iota(shape, 1) // SLOT * 16 + 15)
    per_block = dot(tails, tail_of, 0, 0)
    rank = (iota((128, n * SLOT), 1) % SLOT).astype(jnp.float32)
    filled[...] = jnp.where(rank < per_block, 1.0, 0.0)

    def places(s):
        return one_hot(sublane == from_row[s, 15:16, :].astype(jnp.int32))

    def take(s, carry):
        got = dot(places(s), recv_ref[s], 0, 0).astype(jnp.bfloat16)
        at = pl.ds(pl.multiple_of(s * SLOT, SLOT), SLOT)
        x[:, at, :] = got.reshape(blocks, SLOT, 4 * width)
        return carry

    lax.fori_loop(0, n, take, 0)

    def one(i):
        q = x[i, :, :width]
        k = x[i, :, width:2 * width]
        v = x[i, :, 2 * width:3 * width]
        g = x[i, :, 3 * width:]
        scores = dot(q, k, 1, 1) * scale
        scores = jnp.where(filled[pl.ds(i, 1), :] > 0, scores, masked_score)
        e = jnp.exp(scores - jnp.max(scores, axis=-1, keepdims=True))
        p = e / jnp.sum(e, axis=-1, keepdims=True)
        w = p.astype(jnp.bfloat16)
        dp = dot(g, v, 1, 1)
        delta = jnp.sum(p * dp, axis=-1, keepdims=True)
        ds = (scale * p * (dp - delta)).astype(jnp.bfloat16)
        r[i, :, :width] = dot(w, v).astype(jnp.bfloat16)
        r[i, :, width:2 * width] = dot(ds, k).astype(jnp.bfloat16)
        r[i, :, 2 * width:3 * width] = dot(ds, q, 0, 0).astype(jnp.bfloat16)
        r[i, :, 3 * width:] = dot(w, g, 0, 0).astype(jnp.bfloat16)

    step = 4 if blocks % 4 == 0 and n * SLOT <= 256 else 1

    def attend(i, carry):
        for j in range(step):
            one(i * step + j)
        return carry

    lax.fori_loop(0, blocks // step, attend, 0)

    def give(s, carry):
        at = pl.ds(pl.multiple_of(s * SLOT, SLOT), SLOT)
        rows = r[:, at, :].reshape(slots, 4 * width)
        out_ref[s] = dot(places(s), rows).astype(jnp.bfloat16)
        return carry

    lax.fori_loop(0, n, give, 0)


def unpack_kernel(n, hc, width, window, room, earlier, back_ref, pos_ref, tgt_ref, *refs):
    outs, win = refs[earlier:earlier + 4], refs[-1]
    tokens = outs[0].shape[0]
    place = lax.broadcasted_iota(jnp.int32, (room, hc * window), 0)

    def from_owner(o, carry):
        win[o] = dot(one_hot(place == tgt_ref[o]), back_ref[o], 0, 0).astype(jnp.bfloat16)
        return carry

    lax.fori_loop(0, n, from_owner, 0)
    slot = lax.broadcasted_iota(jnp.int32, (n * window, tokens), 0)
    for h in range(hc):
        rows = win[:, h * window:(h + 1) * window, :].reshape(n * window, 4 * width)
        got = dot(one_hot(slot == pos_ref[h]), rows, 0, 0).astype(jnp.bfloat16)
        for f in range(4):
            outs[f][:, h * width:(h + 1) * width] = got[:, f * width:(f + 1) * width]


def full(shape):
    return pl.BlockSpec(shape, lambda i: (0,) * len(shape))


def shards(n, queries, keys, values, grad_out, cluster_ids):
    tok_rows = queries.shape[0]
    heads = cluster_ids.shape[0]
    width = queries.shape[1] // heads
    k = CLUSTERS // n
    chunks = 2 if heads % 2 == 0 else 1
    hc = heads // chunks
    window = up16(k * CAP)
    room = up16(hc * k * CAP * 5 // 6)
    blocks = hc * k
    four = 4 * width
    params = pltpu.CompilerParams(vmem_limit_bytes=VMEM)

    cl = cluster_ids[:, :, 0]
    head_no = jnp.arange(heads, dtype=jnp.int32)[:, None]
    minor = cl // n
    owner = (cl % n + head_no * minor) % n
    cid = owner * k + minor
    names = jnp.arange(CLUSTERS, dtype=jnp.int32)
    member = (cid[:, :, None] == names).astype(jnp.bfloat16)
    tok = jnp.arange(tok_rows)
    earlier = (tok[:, None] > tok[None, :]).astype(jnp.bfloat16)
    before = jnp.einsum("ts,hsc->htc", earlier, member, preferred_element_type=jnp.float32)
    counts = jnp.sum(member.astype(jnp.float32), axis=1)
    same = (names[:, None] // k == names[None, :] // k) & (names[:, None] < names[None, :])
    start = jnp.sum(counts[:, :, None] * same.astype(jnp.float32), axis=1)
    start = start + (names // k * window).astype(jnp.float32)
    pos = jnp.sum(member.astype(jnp.float32) * (before + start[:, None, :]), axis=2)
    pos = pos.astype(jnp.int32)
    seg = jnp.sum(counts.reshape(chunks, hc, n, k), axis=3).astype(jnp.int32)
    ends = jnp.cumsum(seg, axis=1)
    base = ends - seg
    overflow = (jnp.max(ends) > room - 1).astype(jnp.float32)
    j = jnp.arange(window, dtype=jnp.int32)
    tgt = jnp.where(j < seg[..., None], base[..., None] + j, -1)
    tgt = jnp.swapaxes(tgt, 1, 2).reshape(chunks, n, hc * window)
    cnt_row = jnp.swapaxes(counts.reshape(chunks, hc, n, k), 1, 2).reshape(chunks, n, 1, blocks)
    flag = jnp.broadcast_to(overflow, (chunks, n, 1, 1))
    rest = jnp.zeros((chunks, n, 1, four - blocks - 1), jnp.float32)
    cnt_row = jnp.concatenate([cnt_row, flag, rest], axis=3)

    def pack(c):
        cols = pl.BlockSpec((tok_rows, hc * width), lambda i: (0, c))
        return pl.pallas_call(
            functools.partial(pack_kernel, n, hc, width, window, room),
            grid=(1,),
            out_shape=jax.ShapeDtypeStruct((n, room, four), jnp.bfloat16),
            in_specs=[cols] * 4 + [full((hc, 1, tok_rows)), full((n, 1, hc * window)), full((n, 1, four))],
            out_specs=full((n, room, four)),
            scratch_shapes=[pltpu.VMEM((n, hc * window, four), jnp.bfloat16)],
            compiler_params=params,
            cost_estimate=pl.CostEstimate(flops=6 * 10**9, bytes_accessed=5 * 10**6, transcendentals=0),
        )(queries, keys, values, grad_out,
          pos[c * hc:(c + 1) * hc, None, :], tgt[c][:, None, :], cnt_row[c])

    def work(recv):
        return pl.pallas_call(
            functools.partial(work_kernel, n, blocks, width, room),
            out_shape=jax.ShapeDtypeStruct((n, room, four), jnp.bfloat16),
            scratch_shapes=[pltpu.VMEM((blocks, n * SLOT, four), jnp.bfloat16)] * 2
            + [
                pltpu.VMEM((n, 16, blocks * SLOT), jnp.float32),
                pltpu.VMEM((128, n * SLOT), jnp.float32),
            ],
            compiler_params=params,
            cost_estimate=pl.CostEstimate(flops=10**10, bytes_accessed=5 * 10**6, transcendentals=10**6),
        )(recv)

    def unpack(c, back, so_far):
        wide = jax.ShapeDtypeStruct((tok_rows, heads * width), jnp.bfloat16)
        cols = pl.BlockSpec((tok_rows, hc * width), lambda i: (0, c))
        return pl.pallas_call(
            functools.partial(unpack_kernel, n, hc, width, window, room, len(so_far)),
            grid=(1,),
            out_shape=[wide] * 4,
            in_specs=[full((n, room, four)), full((hc, 1, tok_rows)), full((n, 1, hc * window))]
            + [pl.BlockSpec(memory_space=pl.ANY)] * len(so_far),
            out_specs=[cols] * 4,
            scratch_shapes=[pltpu.VMEM((n, hc * window, four), jnp.bfloat16)],
            input_output_aliases={3 + i: i for i in range(len(so_far))},
            compiler_params=params,
            cost_estimate=pl.CostEstimate(flops=6 * 10**9, bytes_accessed=5 * 10**6, transcendentals=0),
        )(back, pos[c * hc:(c + 1) * hc, None, :], tgt[c][:, None, :], *so_far)

    def exchange(rows):
        return lax.all_to_all(rows, AXES, split_axis=0, concat_axis=0, tiled=True)

    sent = [exchange(pack(c)) for c in range(chunks)]
    normed = unit_rows(keys.reshape(tok_rows, heads, width).astype(jnp.float32))
    own = (cl[:, :, None] == names).astype(jnp.float32)
    partial_sums = jnp.einsum("htc,thd->hcd", own, normed, precision=lax.Precision.HIGHEST)
    centroid_sums = lax.psum(partial_sums, AXES)
    back = [exchange(work(recv)) for recv in sent]
    outs = ()
    for c in range(chunks - 1):
        outs = unpack(c, back[c], tuple(outs))
    outs = lax.cond(
        jnp.max(sent[0][:, room - 1, blocks]) > 0,
        lambda: padded_path(queries, keys, values, grad_out, cluster_ids),
        lambda: tuple(unpack(chunks - 1, back[-1], tuple(outs))),
    )
    return (*outs, centroid_sums)


def solution(mesh):
    n = mesh.shape["seq"] * mesh.shape["sub"]
    rows = P(("groups", "seq", "sub"), "head")
    return jax.shard_map(
        functools.partial(shards, n),
        mesh=mesh,
        in_specs=(rows, rows, rows, rows, P("head", ("groups", "seq", "sub"), None)),
        out_specs=(rows, rows, rows, rows, P("head", "groups", None)),
        check_vma=False,
    )
```

```python
import functools
import jax
import jax.numpy as jnp
from jax import lax
from jax.experimental import pallas as pl
from jax.experimental.pallas import tpu as pltpu
from jax.sharding import PartitionSpec as P

CLUSTERS = 64
CAP = 12
SLOT = 16
AXES = ("seq", "sub")
VMEM = 56 * 1024 * 1024


norm_eps = 1e-06
masked_score = -1e30


def unit_rows(matrix):
    return matrix * lax.rsqrt(jnp.sum(matrix * matrix, axis=-1, keepdims=True) + norm_eps)


def cluster_work(packed, counts):
    head_width = packed.shape[-1] // 4
    row_count = packed.shape[2]
    slot_rank = (jnp.arange(row_count) % CAP).astype(jnp.float32)
    filled = jnp.repeat(counts.astype(jnp.float32), CAP, axis=2)
    filled_slot = slot_rank[None, None, :] < filled
    query_rows = packed[..., :head_width]
    key_rows = packed[..., head_width : 2 * head_width]
    value_rows = packed[..., 2 * head_width : 3 * head_width]
    grad_rows = packed[..., 3 * head_width :]
    score_scale = head_width ** (-0.5)
    scores = (
        jnp.einsum("hcqd,hckd->hcqk", query_rows, key_rows, preferred_element_type=jnp.float32)
        * score_scale
    )
    scores = jnp.where(filled_slot[:, :, None, :], scores, masked_score)
    row_max = jnp.max(scores, axis=-1, keepdims=True)
    exp_scores = jnp.exp(scores - row_max)
    probabilities = exp_scores / jnp.sum(exp_scores, axis=-1, keepdims=True)
    weights = probabilities.astype(jnp.bfloat16)
    attention = jnp.einsum(
        "hcqk,hckd->hcqd", weights, value_rows, preferred_element_type=jnp.float32
    ).astype(jnp.bfloat16)
    dprobs = jnp.einsum(
        "hcqd,hckd->hcqk", grad_rows, value_rows, preferred_element_type=jnp.float32
    )
    row_delta = jnp.sum(probabilities * dprobs, axis=-1, keepdims=True)
    dscore = (score_scale * probabilities * (dprobs - row_delta)).astype(jnp.bfloat16)
    dquery = jnp.einsum(
        "hcqk,hckd->hcqd", dscore, key_rows, preferred_element_type=jnp.float32
    ).astype(jnp.bfloat16)
    dkey = jnp.einsum(
        "hcqk,hcqd->hckd", dscore, query_rows, preferred_element_type=jnp.float32
    ).astype(jnp.bfloat16)
    dvalue = jnp.einsum(
        "hcqk,hcqd->hckd", weights, grad_rows, preferred_element_type=jnp.float32
    ).astype(jnp.bfloat16)
    result = jnp.concatenate([attention, dquery, dkey, dvalue], axis=-1)
    cluster_sums = None
    return (result, cluster_sums)


def padded_path(queries, keys, values, grad_out, cluster_ids):
    tok_rows = queries.shape[0]
    heads_here = cluster_ids.shape[0]
    head_width = queries.shape[1] // heads_here
    cluster_of = cluster_ids[:, :, 0]
    member = (
        cluster_of[:, :, None] == jnp.arange(CLUSTERS, dtype=jnp.int32)[None, None, :]
    ).astype(jnp.int32)
    before = jnp.cumsum(member, axis=1) - member
    slot_rank = jnp.sum(before * member, axis=2)
    slot_index = cluster_of * CAP + slot_rank
    dispatch = (
        slot_index[:, None, :] == jnp.arange(CLUSTERS * CAP, dtype=jnp.int32)[None, :, None]
    ).astype(jnp.bfloat16)
    counts = jnp.sum(member, axis=1).astype(jnp.bfloat16)[:, :, None]
    head_shape = (tok_rows, heads_here, head_width)
    stacked = jnp.stack(
        [
            queries.reshape(head_shape),
            keys.reshape(head_shape),
            values.reshape(head_shape),
            grad_out.reshape(head_shape),
        ],
        axis=2,
    )
    packed = jnp.einsum(
        "hst,thfd->hsfd", dispatch, stacked, preferred_element_type=jnp.float32
    ).astype(jnp.bfloat16)
    packed = packed.reshape(heads_here, CLUSTERS, CAP, 4 * head_width)
    result, _ = cluster_work(
        lax.all_to_all(packed, AXES, split_axis=1, concat_axis=2, tiled=True),
        lax.all_to_all(counts, AXES, split_axis=1, concat_axis=2, tiled=True),
    )
    sent_back = lax.all_to_all(result, AXES, split_axis=2, concat_axis=1, tiled=True)
    rows_back = sent_back.reshape(heads_here, CLUSTERS * CAP, 4, head_width)
    merged = jnp.einsum(
        "hst,hsfd->thfd", dispatch, rows_back, preferred_element_type=jnp.float32
    ).astype(jnp.bfloat16)
    flat_shape = (tok_rows, heads_here * head_width)
    return tuple(merged[:, :, i, :].reshape(flat_shape) for i in range(4))


def up16(x):
    return -(-x // 16) * 16


def one_hot(hit):
    return jnp.where(hit, 1.0, 0.0).astype(jnp.bfloat16)


def dot(a, b, ca=1, cb=0):
    return lax.dot_general(
        a, b, (((ca,), (cb,)), ((), ())), preferred_element_type=jnp.float32
    )


def exchange_kernel(n, sub, hc, chunks, width, window, room,
                    q_ref, k_ref, v_ref, g_ref, pos_ref, tgt_ref, cnt_ref,
                    out_a, out_q, out_k, out_v, tails_ref,
                    send, recv, ret, back, win, x, r, from_row, filled, send_sem, recv_sem):
    outs = (out_a, out_q, out_k, out_v)
    tokens = q_ref.shape[0]
    blocks = hc * (CLUSTERS // n)
    slots = blocks * SLOT
    scale = width ** (-0.5)
    iota = functools.partial(lax.broadcasted_iota, jnp.int32)
    me = lax.axis_index("seq") * sub + lax.axis_index("sub")

    def peer(o):
        return {"seq": o // sub, "sub": o % sub}

    def loop(first, last, body):
        lax.fori_loop(first, last, lambda i, carry: (body(i), carry)[1], 0)

    def ahead(d):
        return lax.rem(me + d, n)

    def behind(d):
        return lax.rem(me + n - d, n)

    def copy(way, c, there, mine):
        source, target = ((send, recv), (ret, back))[way]
        return pltpu.make_async_remote_copy(
            src_ref=source.at[c, there],
            dst_ref=target.at[c, mine],
            send_sem=send_sem.at[way, c, there],
            recv_sem=recv_sem.at[way, c, mine],
            device_id=peer(there),
            device_id_type=pl.DeviceIdType.MESH,
        )

    def launch(way, c, earlier):
        def one(d):
            o = ahead(d)
            if earlier is not None:
                copy(*earlier, o, me).wait_send()
            copy(way, c, o, me).start()

        loop(1, n, one)

    def arrived(way, c, d):
        copy(way, c, ahead(d), behind(d)).wait_recv()

    def pack(c):
        slot = iota((n * window, tokens), 0)
        for h in range(hc):
            at = (c * hc + h) * width
            cols = slice(at, at + width)
            rows = jnp.concatenate(
                [q_ref[:, cols], k_ref[:, cols], v_ref[:, cols], g_ref[:, cols]], axis=1
            )
            got = dot(one_hot(slot == pos_ref[c * hc + h]), rows).astype(jnp.bfloat16)
            win[:, h * window:(h + 1) * window, :] = got.reshape(n, window, 4 * width)
        place = iota((room, hc * window), 0)
        last = iota((room, 4 * width), 0) == room - 1

        def rows_for(o):
            rows = dot(one_hot(place == tgt_ref[c, o]), win[o])
            return jnp.where(last, cnt_ref[c, o], rows).astype(jnp.bfloat16)

        def to_owner(d):
            o = ahead(d)
            send[c, o] = rows_for(o)
            if c == 0:
                copy(0, c, o, me).start()

        loop(1, n, to_owner)
        recv[c, me] = rows_for(me)

    def work(c):
        sublane = iota((room, slots), 0)
        tails = recv[c, :, room - 16:, :128]
        if c == 0:
            tails_ref[...] = tails
        tails = tails.reshape(n * 16, 128)
        lane, block = iota((128, slots), 0), iota((128, slots), 1) // SLOT
        count = dot(tails, one_hot(lane == block))
        first = dot(tails, one_hot(lane < block))
        rank = (iota((n * 16, slots), 1) % SLOT).astype(jnp.float32)
        from_row[...] = jnp.where(rank < count, first + rank, -1.0).reshape(n, 16, slots)
        shape = (n * 16, n * SLOT)
        tail_of = one_hot(iota(shape, 0) == iota(shape, 1) // SLOT * 16 + 15)
        per_block = dot(tails, tail_of, 0, 0)
        rank = (iota((128, n * SLOT), 1) % SLOT).astype(jnp.float32)
        filled[...] = jnp.where(rank < per_block, 1.0, 0.0)

        def places(s):
            return one_hot(sublane.astype(jnp.float32) == from_row[s, 15:16, :])

        def take(s):
            got = dot(places(s), recv[c, s], 0, 0).astype(jnp.bfloat16)
            at = pl.ds(pl.multiple_of(s * SLOT, SLOT), SLOT)
            x[:, at, :] = got.reshape(blocks, SLOT, 4 * width)

        loop(0, n, take)

        def one(i):
            q = x[i, :, :width]
            k = x[i, :, width:2 * width]
            v = x[i, :, 2 * width:3 * width]
            g = x[i, :, 3 * width:]
            scores = dot(q, k, 1, 1) * scale
            scores = jnp.where(filled[pl.ds(i, 1), :] > 0, scores, masked_score)
            e = jnp.exp(scores - jnp.max(scores, axis=-1, keepdims=True))
            p = e / jnp.sum(e, axis=-1, keepdims=True)
            w = p.astype(jnp.bfloat16)
            dp = dot(g, v, 1, 1)
            delta = jnp.sum(p * dp, axis=-1, keepdims=True)
            ds = (scale * p * (dp - delta)).astype(jnp.bfloat16)
            r[i, :, :width] = dot(w, v).astype(jnp.bfloat16)
            r[i, :, width:2 * width] = dot(ds, k).astype(jnp.bfloat16)
            r[i, :, 2 * width:3 * width] = dot(ds, q, 0, 0).astype(jnp.bfloat16)
            r[i, :, 3 * width:] = dot(w, g, 0, 0).astype(jnp.bfloat16)

        step = 4 if blocks % 4 == 0 and n * SLOT <= 256 else 1

        def attend(i):
            for j in range(step):
                one(i * step + j)

        loop(0, blocks // step, attend)

        def rows_for(s):
            at = pl.ds(pl.multiple_of(s * SLOT, SLOT), SLOT)
            rows = r[:, at, :].reshape(slots, 4 * width)
            return dot(places(s), rows).astype(jnp.bfloat16)

        def give(d):
            s = ahead(d)
            ret[c, s] = rows_for(s)

        loop(1, n, give)
        back[c, me] = rows_for(me)

    def unpack(c):
        place = iota((room, hc * window), 0)

        def fill(o):
            hit = one_hot(place == tgt_ref[c, o])
            win[o] = dot(hit, back[c, o], 0, 0).astype(jnp.bfloat16)

        def from_owner(d):
            arrived(1, c, d)
            fill(behind(d))

        fill(me)
        loop(1, n, from_owner)
        slot = iota((n * window, tokens), 0)
        for h in range(hc):
            rows = win[:, h * window:(h + 1) * window, :].reshape(n * window, 4 * width)
            got = dot(one_hot(slot == pos_ref[c * hc + h]), rows, 0, 0).astype(jnp.bfloat16)
            at = (c * hc + h) * width
            for f in range(4):
                outs[f][:, at:at + width] = got[:, f * width:(f + 1) * width]

    barrier = pltpu.get_barrier_semaphore()
    loop(1, n, lambda d: pl.semaphore_signal(
        barrier, inc=1, device_id=peer(ahead(d)), device_id_type=pl.DeviceIdType.MESH
    ))
    pl.semaphore_wait(barrier, n - 1)
    pack(0)
    under_way = (0, 0)
    for c in range(1, chunks):
        pack(c)
        launch(0, c, under_way)
        under_way = (0, c)
    for c in range(chunks):
        loop(1, n, functools.partial(arrived, 0, c))
        work(c)
        launch(1, c, under_way)
        under_way = (1, c)
    for c in range(chunks):
        unpack(c)
    loop(1, n, lambda d: copy(*under_way, ahead(d), me).wait_send())


def shards(n, sub, queries, keys, values, grad_out, cluster_ids):
    tok_rows = queries.shape[0]
    heads = cluster_ids.shape[0]
    width = queries.shape[1] // heads
    k = CLUSTERS // n
    chunks = 2 if heads % 2 == 0 else 1
    hc = heads // chunks
    window = up16(k * CAP)
    room = up16(hc * k * CAP * 5 // 6)
    blocks = hc * k
    four = 4 * width
    params = pltpu.CompilerParams(vmem_limit_bytes=VMEM)

    cl = cluster_ids[:, :, 0]
    head_no = jnp.arange(heads, dtype=jnp.int32)[:, None]
    minor = cl // n
    owner = (cl % n + head_no * minor) % n
    cid = owner * k + minor
    names = jnp.arange(CLUSTERS, dtype=jnp.int32)
    member = (cid[:, :, None] == names).astype(jnp.bfloat16)
    tok = jnp.arange(tok_rows)
    earlier = (tok[:, None] > tok[None, :]).astype(jnp.bfloat16)
    before = jnp.einsum("ts,hsc->htc", earlier, member, preferred_element_type=jnp.float32)
    counts = jnp.sum(member.astype(jnp.float32), axis=1)
    same = (names[:, None] // k == names[None, :] // k) & (names[:, None] < names[None, :])
    start = jnp.sum(counts[:, :, None] * same.astype(jnp.float32), axis=1)
    start = start + (names // k * window).astype(jnp.float32)
    pos = jnp.sum(member.astype(jnp.float32) * (before + start[:, None, :]), axis=2)
    pos = pos.astype(jnp.int32)
    seg = jnp.sum(counts.reshape(chunks, hc, n, k), axis=3).astype(jnp.int32)
    ends = jnp.cumsum(seg, axis=1)
    base = ends - seg
    overflow = (jnp.max(ends) > room - 1).astype(jnp.float32)
    j = jnp.arange(window, dtype=jnp.int32)
    tgt = jnp.where(j < seg[..., None], base[..., None] + j, -1)
    tgt = jnp.swapaxes(tgt, 1, 2).reshape(chunks, n, hc * window)
    cnt_row = jnp.swapaxes(counts.reshape(chunks, hc, n, k), 1, 2).reshape(chunks, n, 1, blocks)
    flag = jnp.broadcast_to(overflow, (chunks, n, 1, 1))
    rest = jnp.zeros((chunks, n, 1, four - blocks - 1), jnp.float32)
    cnt_row = jnp.concatenate([cnt_row, flag, rest], axis=3)

    normed = unit_rows(keys.reshape(tok_rows, heads, width).astype(jnp.float32))
    own = (cl[:, :, None] == names).astype(jnp.float32)
    partial_sums = jnp.einsum("htc,thd->hcd", own, normed, precision=lax.Precision.HIGHEST)
    centroid_sums = lax.psum(partial_sums, AXES)
    wide = jax.ShapeDtypeStruct((tok_rows, heads * width), jnp.bfloat16)
    slots = blocks * SLOT
    parcel = pltpu.VMEM((chunks, n, room, four), jnp.bfloat16)
    *outs, tails = pl.pallas_call(
        functools.partial(exchange_kernel, n, sub, hc, chunks, width, window, room),
        out_shape=[wide] * 4 + [jax.ShapeDtypeStruct((n, 16, 128), jnp.bfloat16)],
        in_specs=[pl.BlockSpec(memory_space=pltpu.VMEM)] * 7,
        out_specs=[pl.BlockSpec(memory_space=pltpu.VMEM)] * 5,
        scratch_shapes=[parcel] * 4
        + [
            pltpu.VMEM((n, hc * window, four), jnp.bfloat16),
            pltpu.VMEM((blocks, n * SLOT, four), jnp.bfloat16),
            pltpu.VMEM((blocks, n * SLOT, four), jnp.bfloat16),
            pltpu.VMEM((n, 16, slots), jnp.float32),
            pltpu.VMEM((128, n * SLOT), jnp.float32),
            pltpu.SemaphoreType.DMA((2, chunks, n)),
            pltpu.SemaphoreType.DMA((2, chunks, n)),
        ],
        compiler_params=pltpu.CompilerParams(
            vmem_limit_bytes=VMEM, collective_id=0, has_side_effects=True
        ),
        cost_estimate=pl.CostEstimate(flops=5 * 10**10, bytes_accessed=10**7, transcendentals=10**6),
    )(queries, keys, values, grad_out, pos[:, None, :], tgt[:, :, None, :], cnt_row)
    outs = lax.cond(
        jnp.max(tails[:, 15, blocks]) > 0,
        lambda: padded_path(queries, keys, values, grad_out, cluster_ids),
        lambda: tuple(outs),
    )
    return (*outs, centroid_sums)


def solution(mesh):
    n = mesh.shape["seq"] * mesh.shape["sub"]
    rows = P(("groups", "seq", "sub"), "head")
    return jax.shard_map(
        functools.partial(shards, n, mesh.shape["sub"]),
        mesh=mesh,
        in_specs=(rows, rows, rows, rows, P("head", ("groups", "seq", "sub"), None)),
        out_specs=(rows, rows, rows, rows, P("head", "groups", None)),
        check_vma=False,
    )
```

```python
import functools
import jax
import jax.numpy as jnp
from jax import lax
from jax.experimental import pallas as pl
from jax.experimental.pallas import tpu as pltpu
from jax.sharding import PartitionSpec as P

CLUSTERS = 64
CAP = 12
SLOT = 16
AXES = ("seq", "sub")
VMEM = 56 * 1024 * 1024


norm_eps = 1e-06
masked_score = -1e30


def unit_rows(matrix):
    return matrix * lax.rsqrt(jnp.sum(matrix * matrix, axis=-1, keepdims=True) + norm_eps)


def cluster_work(packed, counts):
    head_width = packed.shape[-1] // 4
    row_count = packed.shape[2]
    slot_rank = (jnp.arange(row_count) % CAP).astype(jnp.float32)
    filled = jnp.repeat(counts.astype(jnp.float32), CAP, axis=2)
    filled_slot = slot_rank[None, None, :] < filled
    query_rows = packed[..., :head_width]
    key_rows = packed[..., head_width : 2 * head_width]
    value_rows = packed[..., 2 * head_width : 3 * head_width]
    grad_rows = packed[..., 3 * head_width :]
    score_scale = head_width ** (-0.5)
    scores = (
        jnp.einsum("hcqd,hckd->hcqk", query_rows, key_rows, preferred_element_type=jnp.float32)
        * score_scale
    )
    scores = jnp.where(filled_slot[:, :, None, :], scores, masked_score)
    row_max = jnp.max(scores, axis=-1, keepdims=True)
    exp_scores = jnp.exp(scores - row_max)
    probabilities = exp_scores / jnp.sum(exp_scores, axis=-1, keepdims=True)
    weights = probabilities.astype(jnp.bfloat16)
    attention = jnp.einsum(
        "hcqk,hckd->hcqd", weights, value_rows, preferred_element_type=jnp.float32
    ).astype(jnp.bfloat16)
    dprobs = jnp.einsum(
        "hcqd,hckd->hcqk", grad_rows, value_rows, preferred_element_type=jnp.float32
    )
    row_delta = jnp.sum(probabilities * dprobs, axis=-1, keepdims=True)
    dscore = (score_scale * probabilities * (dprobs - row_delta)).astype(jnp.bfloat16)
    dquery = jnp.einsum(
        "hcqk,hckd->hcqd", dscore, key_rows, preferred_element_type=jnp.float32
    ).astype(jnp.bfloat16)
    dkey = jnp.einsum(
        "hcqk,hcqd->hckd", dscore, query_rows, preferred_element_type=jnp.float32
    ).astype(jnp.bfloat16)
    dvalue = jnp.einsum(
        "hcqk,hcqd->hckd", weights, grad_rows, preferred_element_type=jnp.float32
    ).astype(jnp.bfloat16)
    result = jnp.concatenate([attention, dquery, dkey, dvalue], axis=-1)
    cluster_sums = None
    return (result, cluster_sums)


def padded_path(queries, keys, values, grad_out, cluster_ids):
    tok_rows = queries.shape[0]
    heads_here = cluster_ids.shape[0]
    head_width = queries.shape[1] // heads_here
    cluster_of = cluster_ids[:, :, 0]
    member = (
        cluster_of[:, :, None] == jnp.arange(CLUSTERS, dtype=jnp.int32)[None, None, :]
    ).astype(jnp.int32)
    before = jnp.cumsum(member, axis=1) - member
    slot_rank = jnp.sum(before * member, axis=2)
    slot_index = cluster_of * CAP + slot_rank
    dispatch = (
        slot_index[:, None, :] == jnp.arange(CLUSTERS * CAP, dtype=jnp.int32)[None, :, None]
    ).astype(jnp.bfloat16)
    counts = jnp.sum(member, axis=1).astype(jnp.bfloat16)[:, :, None]
    head_shape = (tok_rows, heads_here, head_width)
    stacked = jnp.stack(
        [
            queries.reshape(head_shape),
            keys.reshape(head_shape),
            values.reshape(head_shape),
            grad_out.reshape(head_shape),
        ],
        axis=2,
    )
    packed = jnp.einsum(
        "hst,thfd->hsfd", dispatch, stacked, preferred_element_type=jnp.float32
    ).astype(jnp.bfloat16)
    packed = packed.reshape(heads_here, CLUSTERS, CAP, 4 * head_width)
    result, _ = cluster_work(
        lax.all_to_all(packed, AXES, split_axis=1, concat_axis=2, tiled=True),
        lax.all_to_all(counts, AXES, split_axis=1, concat_axis=2, tiled=True),
    )
    sent_back = lax.all_to_all(result, AXES, split_axis=2, concat_axis=1, tiled=True)
    rows_back = sent_back.reshape(heads_here, CLUSTERS * CAP, 4, head_width)
    merged = jnp.einsum(
        "hst,hsfd->thfd", dispatch, rows_back, preferred_element_type=jnp.float32
    ).astype(jnp.bfloat16)
    flat_shape = (tok_rows, heads_here * head_width)
    return tuple(merged[:, :, i, :].reshape(flat_shape) for i in range(4))


def up16(x):
    return -(-x // 16) * 16


def one_hot(hit):
    return jnp.where(hit, 1.0, 0.0).astype(jnp.bfloat16)


def dot(a, b, ca=1, cb=0):
    return lax.dot_general(
        a, b, (((ca,), (cb,)), ((), ())), preferred_element_type=jnp.float32
    )


def exchange_kernel(n, sub, hc, chunks, width, window, room,
                    q_ref, k_ref, v_ref, g_ref, pos_ref, tgt_ref, cnt_ref,
                    out_a, out_q, out_k, out_v, tails_ref,
                    send, recv, ret, back, win, x, r, from_row, filled, send_sem, recv_sem):
    outs = (out_a, out_q, out_k, out_v)
    tokens = q_ref.shape[0]
    blocks = hc * (CLUSTERS // n)
    slots = blocks * SLOT
    scale = width ** (-0.5)
    iota = functools.partial(lax.broadcasted_iota, jnp.int32)
    me = lax.axis_index("seq") * sub + lax.axis_index("sub")

    def peer(o):
        return {"seq": o // sub, "sub": o % sub}

    def loop(first, last, body):
        lax.fori_loop(first, last, lambda i, carry: (body(i), carry)[1], 0)

    def turn(d):
        return lax.rem(d + n // 2 - 2 + (n - 1), n - 1) + 1

    def ahead(d):
        return lax.rem(me + turn(d), n)

    def behind(d):
        return lax.rem(me + n - turn(d), n)

    def copy(way, c, there, mine):
        source, target = ((send, recv), (ret, back))[way]
        return pltpu.make_async_remote_copy(
            src_ref=source.at[c, there],
            dst_ref=target.at[c, mine],
            send_sem=send_sem.at[way, c, there],
            recv_sem=recv_sem.at[way, c, mine],
            device_id=peer(there),
            device_id_type=pl.DeviceIdType.MESH,
        )

    def launch(way, c, earlier):
        def one(d):
            o = ahead(d)
            if earlier is not None:
                copy(*earlier, o, me).wait_send()
            copy(way, c, o, me).start()

        loop(1, n, one)

    def arrived(way, c, d):
        copy(way, c, ahead(d), behind(d)).wait_recv()

    def pack(c):
        slot = iota((n * window, tokens), 0)
        for h in range(hc):
            at = (c * hc + h) * width
            cols = slice(at, at + width)
            rows = jnp.concatenate(
                [q_ref[:, cols], k_ref[:, cols], v_ref[:, cols], g_ref[:, cols]], axis=1
            )
            got = dot(one_hot(slot == pos_ref[c * hc + h]), rows).astype(jnp.bfloat16)
            win[:, h * window:(h + 1) * window, :] = got.reshape(n, window, 4 * width)
        place = iota((room, hc * window), 0)
        last = iota((room, 4 * width), 0) == room - 1

        def rows_for(o):
            rows = dot(one_hot(place == tgt_ref[c, o]), win[o])
            return jnp.where(last, cnt_ref[c, o], rows).astype(jnp.bfloat16)

        def to_owner(d):
            o = ahead(d)
            send[c, o] = rows_for(o)
            if c == 0:
                copy(0, c, o, me).start()

        loop(1, n, to_owner)
        recv[c, me] = rows_for(me)

    def work(c):
        sublane = iota((room, slots), 0)
        tails = recv[c, :, room - 16:, :128]
        if c == 0:
            tails_ref[...] = tails
        tails = tails.reshape(n * 16, 128)
        lane, block = iota((128, slots), 0), iota((128, slots), 1) // SLOT
        count = dot(tails, one_hot(lane == block))
        first = dot(tails, one_hot(lane < block))
        rank = (iota((n * 16, slots), 1) % SLOT).astype(jnp.float32)
        from_row[...] = jnp.where(rank < count, first + rank, -1.0).reshape(n, 16, slots)
        shape = (n * 16, n * SLOT)
        tail_of = one_hot(iota(shape, 0) == iota(shape, 1) // SLOT * 16 + 15)
        per_block = dot(tails, tail_of, 0, 0)
        rank = (iota((128, n * SLOT), 1) % SLOT).astype(jnp.float32)
        filled[...] = jnp.where(rank < per_block, 1.0, 0.0)

        def places(s):
            return one_hot(sublane.astype(jnp.float32) == from_row[s, 15:16, :])

        def take(s):
            got = dot(places(s), recv[c, s], 0, 0).astype(jnp.bfloat16)
            at = pl.ds(pl.multiple_of(s * SLOT, SLOT), SLOT)
            x[:, at, :] = got.reshape(blocks, SLOT, 4 * width)

        loop(0, n, take)

        def one(i):
            q = x[i, :, :width]
            k = x[i, :, width:2 * width]
            v = x[i, :, 2 * width:3 * width]
            g = x[i, :, 3 * width:]
            scores = dot(q, k, 1, 1) * scale
            scores = jnp.where(filled[pl.ds(i, 1), :] > 0, scores, masked_score)
            e = jnp.exp(scores - jnp.max(scores, axis=-1, keepdims=True))
            p = e / jnp.sum(e, axis=-1, keepdims=True)
            w = p.astype(jnp.bfloat16)
            dp = dot(g, v, 1, 1)
            delta = jnp.sum(p * dp, axis=-1, keepdims=True)
            ds = (scale * p * (dp - delta)).astype(jnp.bfloat16)
            r[i, :, :width] = dot(w, v).astype(jnp.bfloat16)
            r[i, :, width:2 * width] = dot(ds, k).astype(jnp.bfloat16)
            r[i, :, 2 * width:3 * width] = dot(ds, q, 0, 0).astype(jnp.bfloat16)
            r[i, :, 3 * width:] = dot(w, g, 0, 0).astype(jnp.bfloat16)

        step = 4 if blocks % 4 == 0 and n * SLOT <= 256 else 1

        def attend(i):
            for j in range(step):
                one(i * step + j)

        loop(0, blocks // step, attend)

        def rows_for(s):
            at = pl.ds(pl.multiple_of(s * SLOT, SLOT), SLOT)
            rows = r[:, at, :].reshape(slots, 4 * width)
            return dot(places(s), rows).astype(jnp.bfloat16)

        def give(d):
            s = ahead(d)
            ret[c, s] = rows_for(s)

        loop(1, n, give)
        back[c, me] = rows_for(me)

    def unpack(c):
        place = iota((room, hc * window), 0)

        def fill(o):
            hit = one_hot(place == tgt_ref[c, o])
            win[o] = dot(hit, back[c, o], 0, 0).astype(jnp.bfloat16)

        def from_owner(d):
            arrived(1, c, d)
            fill(behind(d))

        fill(me)
        loop(1, n, from_owner)
        slot = iota((n * window, tokens), 0)
        for h in range(hc):
            rows = win[:, h * window:(h + 1) * window, :].reshape(n * window, 4 * width)
            got = dot(one_hot(slot == pos_ref[c * hc + h]), rows, 0, 0).astype(jnp.bfloat16)
            at = (c * hc + h) * width
            for f in range(4):
                outs[f][:, at:at + width] = got[:, f * width:(f + 1) * width]

    barrier = pltpu.get_barrier_semaphore()
    loop(1, n, lambda d: pl.semaphore_signal(
        barrier, inc=1, device_id=peer(ahead(d)), device_id_type=pl.DeviceIdType.MESH
    ))
    pl.semaphore_wait(barrier, n - 1)
    pack(0)
    under_way = (0, 0)
    for c in range(1, chunks):
        pack(c)
        launch(0, c, under_way)
        under_way = (0, c)
    for c in range(chunks):
        loop(1, n, functools.partial(arrived, 0, c))
        work(c)
        launch(1, c, under_way)
        under_way = (1, c)
    for c in range(chunks):
        unpack(c)
    loop(1, n, lambda d: copy(*under_way, ahead(d), me).wait_send())


def shards(n, sub, queries, keys, values, grad_out, cluster_ids):
    tok_rows = queries.shape[0]
    heads = cluster_ids.shape[0]
    width = queries.shape[1] // heads
    k = CLUSTERS // n
    chunks = 2 if heads % 2 == 0 else 1
    hc = heads // chunks
    window = up16(k * CAP)
    room = up16(hc * k * CAP * 5 // 6)
    blocks = hc * k
    four = 4 * width
    params = pltpu.CompilerParams(vmem_limit_bytes=VMEM)

    cl = cluster_ids[:, :, 0]
    head_no = jnp.arange(heads, dtype=jnp.int32)[:, None]
    minor = cl // n
    owner = (cl % n + head_no * minor) % n
    cid = owner * k + minor
    names = jnp.arange(CLUSTERS, dtype=jnp.int32)
    member = (cid[:, :, None] == names).astype(jnp.bfloat16)
    tok = jnp.arange(tok_rows)
    earlier = (tok[:, None] > tok[None, :]).astype(jnp.bfloat16)
    before = jnp.einsum("ts,hsc->htc", earlier, member, preferred_element_type=jnp.float32)
    counts = jnp.sum(member.astype(jnp.float32), axis=1)
    same = (names[:, None] // k == names[None, :] // k) & (names[:, None] < names[None, :])
    start = jnp.sum(counts[:, :, None] * same.astype(jnp.float32), axis=1)
    start = start + (names // k * window).astype(jnp.float32)
    pos = jnp.sum(member.astype(jnp.float32) * (before + start[:, None, :]), axis=2)
    pos = pos.astype(jnp.int32)
    seg = jnp.sum(counts.reshape(chunks, hc, n, k), axis=3).astype(jnp.int32)
    ends = jnp.cumsum(seg, axis=1)
    base = ends - seg
    overflow = (jnp.max(ends) > room - 1).astype(jnp.float32)
    j = jnp.arange(window, dtype=jnp.int32)
    tgt = jnp.where(j < seg[..., None], base[..., None] + j, -1)
    tgt = jnp.swapaxes(tgt, 1, 2).reshape(chunks, n, hc * window)
    cnt_row = jnp.swapaxes(counts.reshape(chunks, hc, n, k), 1, 2).reshape(chunks, n, 1, blocks)
    flag = jnp.broadcast_to(overflow, (chunks, n, 1, 1))
    rest = jnp.zeros((chunks, n, 1, four - blocks - 1), jnp.float32)
    cnt_row = jnp.concatenate([cnt_row, flag, rest], axis=3)

    normed = unit_rows(keys.reshape(tok_rows, heads, width).astype(jnp.float32))
    own = (cl[:, :, None] == names).astype(jnp.float32)
    partial_sums = jnp.einsum("htc,thd->hcd", own, normed, precision=lax.Precision.HIGHEST)
    centroid_sums = lax.psum(partial_sums, AXES)
    wide = jax.ShapeDtypeStruct((tok_rows, heads * width), jnp.bfloat16)
    slots = blocks * SLOT
    parcel = pltpu.VMEM((chunks, n, room, four), jnp.bfloat16)
    *outs, tails = pl.pallas_call(
        functools.partial(exchange_kernel, n, sub, hc, chunks, width, window, room),
        out_shape=[wide] * 4 + [jax.ShapeDtypeStruct((n, 16, 128), jnp.bfloat16)],
        in_specs=[pl.BlockSpec(memory_space=pltpu.VMEM)] * 7,
        out_specs=[pl.BlockSpec(memory_space=pltpu.VMEM)] * 5,
        scratch_shapes=[parcel] * 4
        + [
            pltpu.VMEM((n, hc * window, four), jnp.bfloat16),
            pltpu.VMEM((blocks, n * SLOT, four), jnp.bfloat16),
            pltpu.VMEM((blocks, n * SLOT, four), jnp.bfloat16),
            pltpu.VMEM((n, 16, slots), jnp.float32),
            pltpu.VMEM((128, n * SLOT), jnp.float32),
            pltpu.SemaphoreType.DMA((2, chunks, n)),
            pltpu.SemaphoreType.DMA((2, chunks, n)),
        ],
        compiler_params=pltpu.CompilerParams(
            vmem_limit_bytes=VMEM, collective_id=0, has_side_effects=True
        ),
        cost_estimate=pl.CostEstimate(flops=5 * 10**10, bytes_accessed=10**7, transcendentals=10**6),
    )(queries, keys, values, grad_out, pos[:, None, :], tgt[:, :, None, :], cnt_row)
    outs = lax.cond(
        jnp.max(tails[:, 15, blocks]) > 0,
        lambda: padded_path(queries, keys, values, grad_out, cluster_ids),
        lambda: tuple(outs),
    )
    return (*outs, centroid_sums)


def solution(mesh):
    n = mesh.shape["seq"] * mesh.shape["sub"]
    rows = P(("groups", "seq", "sub"), "head")
    return jax.shard_map(
        functools.partial(shards, n, mesh.shape["sub"]),
        mesh=mesh,
        in_specs=(rows, rows, rows, rows, P("head", ("groups", "seq", "sub"), None)),
        out_specs=(rows, rows, rows, rows, P("head", "groups", None)),
        check_vma=False,
    )
```
